32 devices in a mesh: groups: 2 (over y), ep: 4 (over z), tp: 4 (over x, core).
Axes of the slice: x: 2, y: 2, z: 4, core: 2. Of those that a mesh axis runs over, the one named last changes fastest.
Arguments:
- activations: bfloat16 [1024, 16384], P(('groups', 'ep'), 'tp'), parts along dimension 0, may hold values from -6 to 6
- token_expert_index: int32 [1024, 2], P(('groups', 'ep')), parts along dimension 0, may hold values from 0 to 7, all different within a row; in each aligned block of 128 rows (0 to 127, 128 to 255, ...) at most 40 rows name the same one
- gate_integer_weights: int32 [1024, 2], P(('groups', 'ep')), parts along dimension 0, may hold values from 8192 to 65535
- weight: bfloat16 [8, 16384, 3072], P('ep', 'tp'), may hold values from -2 to 2
- left_reducing_matrices: bfloat16 [8, 16384, 16], P(None, 'tp'), may hold values from -0.046875 to 0.046875
- right_widening_matrices: bfloat16 [8, 16, 3072], P('ep'), may hold values from -0.29882812 to 0.29882812
- magnitude: float32 [8, 3072], P('ep'), may hold values from 0.5 to 2
Outputs:
- projected: bfloat16 [1024, 1, 3072], P(('groups', 'ep'), None, 'tp'), parts along dimension 0
The draws below stay inside these ranges and needn't reach their ends.
There are 2 independent parts, one for each index of `groups`. The reference program is written for one: setup_inputs(seed, part) draws one part's arguments, and reference() takes and returns one part's arrays. A program takes and returns all parts, laid end to end along the dimension named above; an argument that names none is the same for every part. Nothing has to cross between parts.
Inputs may be any that keep to these rules, and one draw needn't show every extreme that they name: `token_expert_index`: the two experts of a token differ. Among the rows of one index of ep no expert is named by more than 40 rows, a bound that some block reaches.
All inputs are finite; a program needn't handle non-finite values.
Results may differ from the reference program's by a relative error of at most 0.014.
Values may be sent and summed in bfloat16 or wider, within the bound.
A program may use at most 128 MiB of HBM per device.

```python
import math
import jax
import jax.numpy as jnp
import numpy as np
from jax import lax

SPECIALISTS = 8
INNER_DIMENSION = 16384
TARGET_DIMENSION = 3072
ADAPTIVE_DEGREE = 16
TOK_DEV = 128
CAP = 40
TOKENS = 512
TILES_PER_MODEL = 1
GLOBAL_TILE_SPAN = 8
TILE_WIDTH = 3072
N_EP = 4


def draw_weight(key, part):
    key = jax.random.fold_in(key, 11)
    key_rows, key_cols, key_main = jax.random.split(key, 3)
    row_level = jax.random.uniform(key_rows, (GLOBAL_TILE_SPAN, INNER_DIMENSION, 1), jnp.float32)
    ramp = jnp.power(3.0, jnp.arange(INNER_DIMENSION, dtype=jnp.float32) / INNER_DIMENSION)
    row_scale = jnp.exp(row_level * math.log(10.0)) * ramp[None, :, None]
    col_level = jax.random.uniform(key_cols, (GLOBAL_TILE_SPAN, 1, TILE_WIDTH), jnp.float32)
    col_scale = jnp.exp(col_level * math.log(10.0))
    entries = jnp.clip(jax.random.normal(key_main, (GLOBAL_TILE_SPAN, INNER_DIMENSION, TILE_WIDTH), jnp.float32), -5.0, 5.0)
    values = entries * row_scale * col_scale / (40.0 * math.sqrt(INNER_DIMENSION))
    return jnp.clip(values, -2.0, 2.0).astype(jnp.bfloat16)


def plant(drawn, rng, smallest, high):
    spot = [jax.random.randint(jax.random.fold_in(rng, axis), (), 0, length) for axis, length in enumerate(drawn.shape)]
    longest = drawn.shape.index(max(drawn.shape))
    beside = spot[:longest] + [(spot[longest] + 1) % drawn.shape[longest]] + spot[longest + 1:]
    return drawn.at[tuple(spot)].set(smallest).at[tuple(beside)].set(high)


def block_scale(own_key, shape, pieces, low, high):
    gain, own = 1.0, jax.random.fold_in(own_key, 6)
    for dim, parts in pieces:
        steps = jnp.exp(jax.random.uniform(jax.random.fold_in(own, dim), (parts,), jnp.float32, low / len(pieces), high / len(pieces)))
        gain = gain * jnp.repeat(steps, shape[dim] // parts).reshape([-1 if axis == dim else 1 for axis in range(len(shape))])
    return gain


def deal_out(rng, own, number, rows, amount, top, most, slope):
    ranking = jax.random.permutation(rng, amount)
    crowded, ordinary = shares(amount, rows * top, most, slope, True), shares(amount, rows * top, most, slope, False)
    places = jnp.arange(amount)

    def named(tallies, offset_by):
        used = int((tallies > 0).sum())
        fixed = max(1, used // 4)
        shifted = fixed + (places - fixed + offset_by * (used - fixed)) % max(1, amount - fixed)
        return jnp.zeros((amount,), jnp.int32).at[ranking[jnp.where(places < fixed, places, shifted)]].set(jnp.asarray(tallies, jnp.int32))

    tallies = jnp.where(number % 4 == 0, named(crowded, number // 4), named(ordinary, number - number // 4 - 1))
    mixed = jax.random.permutation(jax.random.fold_in(own, 3), amount)
    donor, taker = mixed[0:amount // 2 * 2:2], mixed[1:amount // 2 * 2:2]
    slack = jnp.minimum(tallies[donor] - 1, most - tallies[taker]) // 2
    slack = jnp.where((donor == ranking[0]) | (taker == ranking[0]) | (tallies[taker] == 0), 0, jnp.maximum(slack, 0))
    shifted = jax.random.randint(jax.random.fold_in(own, 4), (amount // 2,), 0, 1 << 20) % (slack + 1)
    tallies = tallies.at[donor].add(-shifted).at[taker].add(shifted)
    items = jnp.searchsorted(jnp.cumsum(tallies), jnp.arange(rows * top), side="right").astype(jnp.int32)
    listing = items.reshape(top, rows).T
    listing = listing[jax.random.permutation(jax.random.fold_in(own, 1), rows)]
    offset_by = jax.random.randint(jax.random.fold_in(own, 2), (rows, 1), 0, top)
    return jnp.take_along_axis(listing, (jnp.arange(top)[None, :] + offset_by) % top, axis=1)


def shares(amount, total, most, skew, full):
    weights = [(1 << 20) // math.isqrt(grade ** skew) + 1 for grade in range(1, amount + 1)]
    largest = most if full else min(most, max(-(-total // amount), total * weights[0] // sum(weights)))
    least = 1 if total - largest >= amount - 1 else 0
    holding, spare = [largest] + [least] * (amount - 1), total - largest - least * (amount - 1)
    while spare > 0:
        candidates = [i for i in range(1, amount) if holding[i] < largest] or [i for i in range(1, amount) if holding[i] < most]
        pool, remaining = sum([weights[i] for i in candidates]), spare
        for i in candidates:
            extra = min(most - holding[i], max(1, remaining * weights[i] // pool), spare)
            holding[i] = holding[i] + extra
            spare = spare - extra
    return np.array(holding)


def bell_draw(own_key, extent, scale, bound, cuts=(), kind=jnp.bfloat16):
    result = jax.random.normal(own_key, extent, jnp.float32) * scale
    if len(cuts) > 0:
        result = block_scale(own_key, extent, cuts, -0.22, 0.18) * result
    return jnp.clip(result, min=-bound, max=bound).astype(kind)


def setup_inputs(seed: int = 0, part: int = 0) -> dict:
    seeds = jax.random.split(jax.random.key(seed), 8)
    own_keys = jax.random.split(jax.random.fold_in(seeds[7], part), 8)
    activations = bell_draw(own_keys[0], (TOKENS, INNER_DIMENSION), 1.0, 6.0, ((0, 4), (1, 4)))
    token_expert_index_keys = jax.random.split(jax.random.fold_in(own_keys[1], 1), TOKENS // TOK_DEV)
    token_expert_index_turns = jax.random.permutation(jax.random.fold_in(own_keys[1], 3), TOKENS // TOK_DEV)
    token_expert_index = jax.vmap(lambda own, number: deal_out(jax.random.fold_in(own_keys[1], 2), own, number, TOK_DEV, SPECIALISTS, 2, CAP, 2))(token_expert_index_keys, token_expert_index_turns).reshape((TOKENS, 2))
    gate_integer_weights = plant(jax.random.randint(own_keys[2], (TOKENS, 2), 8192, 65536), jax.random.fold_in(own_keys[2], 1), 8192, 65535).astype(jnp.int32)
    weight = draw_weight(jax.random.fold_in(seeds[7], 71), part)
    left_reducing_matrices = bell_draw(seeds[4], (SPECIALISTS, INNER_DIMENSION, ADAPTIVE_DEGREE), INNER_DIMENSION ** -0.5, 0.046875, ((1, 4),))
    right_widening_matrices = bell_draw(seeds[5], (GLOBAL_TILE_SPAN, ADAPTIVE_DEGREE, TILE_WIDTH), 0.05, 0.29882812, ((0, 4),))
    magnitude = jnp.clip(jnp.exp(math.log(2.0) - 1.3862944 * jax.random.uniform(seeds[6], (GLOBAL_TILE_SPAN, TILE_WIDTH), jnp.float32) ** block_scale(seeds[6], (GLOBAL_TILE_SPAN, TILE_WIDTH), ((0, 4),), -0.2, 0.2)), 0.5, 2.0)
    return dict(activations=activations, token_expert_index=token_expert_index, gate_integer_weights=gate_integer_weights, weight=weight, left_reducing_matrices=left_reducing_matrices, right_widening_matrices=right_widening_matrices, magnitude=magnitude)


def reference(activations, token_expert_index, gate_integer_weights, weight, left_reducing_matrices, right_widening_matrices, magnitude):
    flat = token_expert_index.reshape(-1)
    gate_real = gate_integer_weights.reshape(-1).astype(jnp.float32) / 65536.0
    padded = jnp.concatenate([activations, jnp.zeros((1, INNER_DIMENSION), activations.dtype)], 0)
    w_all = weight.reshape(SPECIALISTS, TILES_PER_MODEL, INNER_DIMENSION, TILE_WIDTH)
    widening_matrix_complete = right_widening_matrices.reshape(SPECIALISTS, TILES_PER_MODEL, ADAPTIVE_DEGREE, TILE_WIDTH)
    m_all = magnitude.reshape(SPECIALISTS, TILES_PER_MODEL * TILE_WIDTH)
    slot_rows = N_EP * CAP
    limit = 2 * TOKENS

    def step(total, specialist_position):
        picked = jnp.nonzero(flat == specialist_position, size=slot_rows, fill_value=limit)[0].astype(jnp.int32)
        token_index = (picked // 2).astype(jnp.int32)
        safe = jnp.minimum(picked, limit - 1).astype(jnp.int32)
        gate_here = jnp.where(picked < limit, gate_real[safe], jnp.float32(0.0))
        chosen = padded[token_index]
        w_exp = jnp.transpose(w_all[specialist_position], (1, 0, 2)).reshape(INNER_DIMENSION, TARGET_DIMENSION)
        widening_matrix_specialist = jnp.transpose(widening_matrix_complete[specialist_position], (1, 0, 2)).reshape(ADAPTIVE_DEGREE, TARGET_DIMENSION)
        expert_down_factor = left_reducing_matrices[specialist_position]
        merged = w_exp.astype(jnp.float32) + 2.0 * jnp.dot(expert_down_factor, widening_matrix_specialist, preferred_element_type=jnp.float32)
        colnorm = jnp.sqrt(lax.optimization_barrier(jnp.sum(merged * merged, axis=0)) + 1e-06)
        low_rank_output = jnp.dot(chosen, expert_down_factor, preferred_element_type=jnp.float32).astype(jnp.bfloat16)
        base_output = jnp.dot(chosen, w_exp, preferred_element_type=jnp.float32)
        branch = (base_output + 2.0 * jnp.dot(low_rank_output, widening_matrix_specialist, preferred_element_type=jnp.float32)) * (m_all[specialist_position] / colnorm)[None, :]
        return (total.at[token_index].add(gate_here[:, None] * branch), None)
    total, _ = lax.scan(step, jnp.zeros((TOKENS + 1, TARGET_DIMENSION), jnp.float32), jnp.arange(SPECIALISTS))
    return total[:TOKENS].reshape(TOKENS, TILES_PER_MODEL, TILE_WIDTH).astype(jnp.bfloat16)
```

```python
import functools

import jax
import jax.numpy as jnp
from jax import lax
from jax.experimental import pallas as pl
from jax.experimental.pallas import tpu as pltpu
from jax.sharding import PartitionSpec as P

CAP = 40
KC = 256
TN = 256
NB = 3
LEAD = 3
F32 = jnp.float32
BF16 = jnp.bfloat16


def dispatch_kernel(
    n, units, blocks, rp, nc,
    x_ref, tgt_ref, w_ref, e_ref, b_ref,
    y_ref, sq_ref,
    gath, land, relay, tg, place, lhs, wbuf, acc, low, sqa,
    t_send, t_recv, send, recv, wsem,
):
    me = lax.axis_index("ep")
    tok = x_ref.shape[0]
    width = w_ref.shape[2]
    rank = b_ref.shape[0] // units
    rows = n * rp
    is_end = jnp.logical_or(me == 0, me == n - 1)

    def w_copy(c, u):
        slot = lax.rem(c, NB)
        return pltpu.make_async_copy(
            w_ref.at[u, pl.ds(pl.multiple_of(c * KC, KC), KC), :],
            wbuf.at[slot, pl.ds(u * KC, KC), :],
            wsem.at[slot, u],
        )

    for c in range(min(NB - 1, nc)):
        for u in range(units):
            w_copy(jnp.int32(c), u).start()

    barrier = pltpu.get_barrier_semaphore()

    def greet(d, _):
        pl.semaphore_signal(barrier, inc=1, device_id={"ep": lax.rem(me + d, n)})
        return 0

    lax.fori_loop(1, n, greet, 0)
    pl.semaphore_wait(barrier, n - 1)

    def remote(src, dst, slot, s, c, to):
        return pltpu.make_async_remote_copy(
            src_ref=src, dst_ref=dst, send_sem=send.at[slot, c], recv_sem=recv.at[s, c],
            device_id={"ep": to},
        )

    def own_cols(c):
        return pl.ds(pl.multiple_of(c * KC, KC), KC)

    def own_full(c, slot, to):
        return remote(x_ref.at[:, own_cols(c)], gath.at[me, c], slot, me, c, to)

    def fwd_full(s, c, to):
        return remote(gath.at[s, c], gath.at[s, c], s, s, c, to)

    def packed(s, slot, c, to):
        return remote(relay.at[slot, c], land.at[s, c], slot, s, c, to)

    def pack(role, s, value):
        return jnp.dot(place[role, s], value, preferred_element_type=F32)

    def own_send_full(c):
        @pl.when(me < n - 2)
        def _():
            own_full(c, me, me + 1).start()

        @pl.when(me > 1)
        def _():
            own_full(c, n, me - 1).start()

    def own_send_packed(c):
        @pl.when(me == n - 2)
        def _():
            relay[me, c] = pack(1, me, x_ref[:, own_cols(c)]).astype(BF16)
            packed(me, me, c, n - 1).start()

        @pl.when(me == 1)
        def _():
            relay[n, c] = pack(2, me, x_ref[:, own_cols(c)]).astype(BF16)
            packed(me, n, c, 0).start()

    lead = min(LEAD, nc)

    def tell(to):
        return pltpu.make_async_remote_copy(
            src_ref=tgt_ref, dst_ref=tg.at[me], send_sem=t_send.at[to], recv_sem=t_recv.at[me],
            device_id={"ep": to},
        )

    def hear(s):
        return pltpu.make_async_remote_copy(
            src_ref=tgt_ref, dst_ref=tg.at[s], send_sem=t_send.at[s], recv_sem=t_recv.at[s],
            device_id={"ep": s},
        )

    def start_tell(d, _):
        tell(lax.rem(me + d, n)).start()
        return 0

    lax.fori_loop(1, n, start_tell, 0)
    for c in range(lead):
        own_send_full(jnp.int32(c))
    tg[me] = tgt_ref[...]

    row = lax.broadcasted_iota(jnp.int32, (rp, tok), 0)

    def wanted(dest):
        val = jnp.full((rp, tok), -1, jnp.int32)
        for u in range(units):
            e = (dest * units + u) // blocks
            inside = jnp.logical_and(row >= u * CAP, row < (u + 1) * CAP)
            val = jnp.where(inside, row + (e * CAP - u * CAP), val)
        return val

    def build(s):
        t = tg[s]
        for role, dest in enumerate((me, n - 1, 0)):
            val = wanted(dest)
            hit = jnp.logical_or(t[0:1, :] == val, t[1:2, :] == val)
            place[role, s] = jnp.where(hit, 1.0, 0.0).astype(BF16)

    build(me)
    for c in range(lead):
        own_send_packed(jnp.int32(c))

    acc[...] = jnp.zeros_like(acc)
    low[...] = jnp.zeros_like(low)
    sqa[...] = jnp.zeros_like(sqa)

    def others(d, _):
        s = lax.rem(me + d, n)
        hear(s).wait_recv()
        build(s)
        return 0

    lax.fori_loop(1, n, others, 0)

    mrow = lax.broadcasted_iota(jnp.int32, (rp, KC), 0)

    def put(s, value):
        at = pl.ds(pl.multiple_of(s * rp, 16), rp)
        for u in range(units):
            mine = jnp.logical_and(mrow >= u * CAP, mrow < (u + 1) * CAP)
            lhs[at, pl.ds(u * KC, KC)] = jnp.where(mine, value, 0.0).astype(BF16)

    def arrive(s, c):
        @pl.when(is_end)
        def _():
            packed(s, s, c, s).wait_recv()
            put(s, land[s, c].astype(F32))

        @pl.when(jnp.logical_not(is_end))
        def _():
            fwd_full(s, c, s).wait_recv()

            @pl.when(s < me)
            def _():
                @pl.when(me < n - 2)
                def _():
                    fwd_full(s, c, me + 1).start()

                @pl.when(me == n - 2)
                def _():
                    relay[s, c] = pack(1, s, gath[s, c]).astype(BF16)
                    packed(s, s, c, n - 1).start()

            @pl.when(s > me)
            def _():
                @pl.when(me > 1)
                def _():
                    fwd_full(s, c, me - 1).start()

                @pl.when(me == 1)
                def _():
                    relay[s, c] = pack(2, s, gath[s, c]).astype(BF16)
                    packed(s, s, c, 0).start()

            put(s, pack(0, s, gath[s, c]))

    def step(c, _):
        @pl.when(c + (NB - 1) < nc)
        def _():
            for u in range(units):
                w_copy(c + (NB - 1), u).start()

        @pl.when(c + lead < nc)
        def _():
            own_send_full(c + lead)
            own_send_packed(c + lead)

        def by_distance(d, _):
            @pl.when(me - d >= 0)
            def _():
                arrive(me - d, c)

            @pl.when(me + d < n)
            def _():
                arrive(me + d, c)

            return 0

        lax.fori_loop(1, n, by_distance, 0)
        put(me, pack(0, me, x_ref[:, own_cols(c)]))
        lhs[pl.ds(rows, units * rank), :] = e_ref[c]
        for u in range(units):
            w_copy(c, u).wait()
        slot = lax.rem(c, NB)

        def tile(j, _):
            cols = pl.ds(pl.multiple_of(j * TN, TN), TN)
            acc[:, cols] += jnp.dot(lhs[...], wbuf[slot, :, cols], preferred_element_type=F32)
            for u in range(units):
                w = wbuf[slot, pl.ds(u * KC, KC), cols].astype(F32)
                sqa[u, :, cols] += jnp.sum((w * w).reshape(KC // 8, 8, TN), axis=0)
            return 0

        lax.fori_loop(0, width // TN, tile, 0)
        low[...] += lax.dot_general(
            lhs[...], e_ref[c], (((1,), (1,)), ((), ())), preferred_element_type=F32
        )
        return 0

    lax.fori_loop(0, nc, step, 0)

    low_rows = low[pl.ds(0, rows), :].astype(BF16)
    gram = low[pl.ds(rows, units * rank), :]

    def finish(j, _):
        cols = pl.ds(pl.multiple_of(j * TN, TN), TN)
        b = b_ref[:, cols]
        y_ref[:, cols] = (
            acc[pl.ds(0, rows), cols] + 2.0 * jnp.dot(low_rows, b, preferred_element_type=F32)
        ).astype(BF16)
        bf = b.astype(F32)
        inner = acc[pl.ds(rows, units * rank), cols] + jnp.dot(
            gram, bf, precision=lax.Precision.HIGHEST, preferred_element_type=F32
        )
        cross = bf * inner
        for u in range(units):
            base = jnp.sum(sqa[u, :, cols], axis=0, keepdims=True)
            extra = jnp.sum(cross[u * rank:(u + 1) * rank], axis=0, keepdims=True)
            sq_ref[u:u + 1, cols] = base + 4.0 * extra
        return 0

    lax.fori_loop(0, width // TN, finish, 0)

    def done_tell(d, _):
        tell(lax.rem(me + d, n)).wait_send()
        return 0

    lax.fori_loop(1, n, done_tell, 0)

    def drain(c, _):
        @pl.when(me < n - 2)
        def _():
            own_full(c, me, me + 1).wait_send()

        @pl.when(me == n - 2)
        def _():
            packed(me, me, c, n - 1).wait_send()

        @pl.when(me > 1)
        def _():
            own_full(c, n, me - 1).wait_send()

        @pl.when(me == 1)
        def _():
            packed(me, n, c, 0).wait_send()

        def sent(s, _):
            @pl.when(jnp.logical_and(s < me, me < n - 2))
            def _():
                fwd_full(s, c, me + 1).wait_send()

            @pl.when(jnp.logical_and(s < me, me == n - 2))
            def _():
                packed(s, s, c, n - 1).wait_send()

            @pl.when(jnp.logical_and(s > me, me > 1))
            def _():
                fwd_full(s, c, me - 1).wait_send()

            @pl.when(jnp.logical_and(s > me, me == 1))
            def _():
                packed(s, s, c, 0).wait_send()

            return 0

        @pl.when(jnp.logical_not(is_end))
        def _():
            lax.fori_loop(0, n, sent, 0)

        return 0

    lax.fori_loop(0, nc, drain, 0)


def routed_products(activations, target, weight, mine, widening, n, blocks):
    tok, feat = activations.shape
    units, _, width = weight.shape
    rank = mine.shape[2]
    rp = -(-units * CAP // 16) * 16
    nc = feat // KC
    rows = n * rp
    low_t = mine.reshape(units, nc, KC, rank).transpose(1, 0, 3, 2)
    diag = jnp.eye(units, dtype=BF16)
    e_all = (low_t[:, :, :, None, :] * diag[None, :, None, :, None]).reshape(
        nc, units * rank, units * KC
    )
    b_all = widening.reshape(units * rank, width)
    targets = jnp.pad(target.T, ((0, 6), (0, 0)), constant_values=-2)
    vmem = pl.BlockSpec(memory_space=pltpu.VMEM)
    return pl.pallas_call(
        functools.partial(dispatch_kernel, n, units, blocks, rp, nc),
        out_shape=(
            jax.ShapeDtypeStruct((rows, width), BF16),
            jax.ShapeDtypeStruct((8, width), F32),
        ),
        in_specs=[vmem, vmem, pl.BlockSpec(memory_space=pl.ANY), vmem, vmem],
        out_specs=(vmem, vmem),
        scratch_shapes=[
            pltpu.VMEM((n, nc, tok, KC), BF16),
            pltpu.VMEM((n, nc, rp, KC), BF16),
            pltpu.VMEM((n + 1, nc, rp, KC), BF16),
            pltpu.VMEM((n, 8, tok), jnp.int32),
            pltpu.VMEM((3, n, rp, tok), BF16),
            pltpu.VMEM((rows + units * rank, units * KC), BF16),
            pltpu.VMEM((NB, units * KC, width), BF16),
            pltpu.VMEM((rows + units * rank, width), F32),
            pltpu.VMEM((rows + units * rank, units * rank), F32),
            pltpu.VMEM((units, 8, width), F32),
            pltpu.SemaphoreType.DMA((n,)),
            pltpu.SemaphoreType.DMA((n,)),
            pltpu.SemaphoreType.DMA((n + 1, nc)),
            pltpu.SemaphoreType.DMA((n, nc)),
            pltpu.SemaphoreType.DMA((NB, units)),
        ],
        compiler_params=pltpu.CompilerParams(
            collective_id=0, has_side_effects=True, vmem_limit_bytes=60 * 1024 * 1024
        ),
        cost_estimate=pl.CostEstimate(
            flops=2 * rows * feat * width, bytes_accessed=2 * units * feat * width, transcendentals=0
        ),
        name="routed_products",
    )(activations, targets, weight, e_all, b_all)


def on_device(
    activations,
    token_expert_index,
    gate_integer_weights,
    weight,
    left_reducing_matrices,
    right_widening_matrices,
    magnitude,
):
    ep_count = lax.axis_size("ep")
    tok_count = activations.shape[0]
    units_here = weight.shape[0]
    expert_list = left_reducing_matrices.shape[0]
    blocks = units_here * ep_count // expert_list
    flat = token_expert_index.reshape(-1)
    onehot = (flat[:, None] == jnp.arange(expert_list, dtype=jnp.int32)[None, :]).astype(jnp.int32)
    before = jnp.cumsum(onehot, axis=0) - onehot
    slot = jnp.sum(before * onehot, axis=1)
    target = (flat * CAP + slot).reshape(tok_count, 2)
    slot_total = expert_list * CAP
    match = jnp.arange(slot_total, dtype=jnp.int32)[:, None, None] == target[None, :, :]
    first_unit = lax.axis_index("ep") * units_here
    mine = jnp.stack(
        [
            lax.dynamic_index_in_dim(
                left_reducing_matrices, (first_unit + unit) // blocks, 0, keepdims=False
            )
            for unit in range(units_here)
        ],
        axis=0,
    )
    partial_rows, squares = routed_products(
        activations, target, weight, mine, right_widening_matrices, ep_count, blocks
    )
    total_sq = jnp.maximum(lax.psum(squares[:units_here], "tp"), 0.0)
    col_scale = magnitude / jnp.sqrt(total_sq + 1e-06)
    gate_real = gate_integer_weights.astype(F32) / 65536.0
    combiner = jnp.sum(match.astype(F32) * gate_real[None, :, :], axis=-1).T
    summed = lax.psum_scatter(partial_rows, "tp", scatter_dimension=1, tiled=True).astype(F32)
    width = summed.shape[1]
    summed = summed.reshape(ep_count, -1, width)[:, : units_here * CAP].reshape(
        ep_count, units_here, CAP, width
    )
    scale_part = lax.dynamic_slice_in_dim(col_scale, lax.axis_index("tp") * width, width, 1)
    back = lax.all_to_all(
        (summed * scale_part[None, :, None, :]).astype(BF16),
        "ep",
        split_axis=0,
        concat_axis=0,
        tiled=True,
    ).astype(F32)
    table = (
        back.reshape(expert_list, blocks, CAP, width)
        .transpose(0, 2, 1, 3)
        .reshape(slot_total, blocks * width)
    )
    mixed = jnp.dot(combiner, table, precision=lax.Precision.HIGHEST).reshape(
        tok_count, blocks, width
    )
    return mixed.astype(BF16)


def solution(mesh):
    return jax.shard_map(
        on_device,
        mesh=mesh,
        in_specs=(
            P(("groups", "ep"), "tp"),
            P(("groups", "ep"), None),
            P(("groups", "ep"), None),
            P("ep", "tp", None),
            P(None, "tp", None),
            P("ep", None, None),
            P("ep", None),
        ),
        out_specs=P(("groups", "ep"), None, "tp"),
        check_vma=False,
    )
```

```python
import functools

import jax
import jax.numpy as jnp
from jax import lax
from jax.experimental import pallas as pl
from jax.experimental.pallas import tpu as pltpu
from jax.sharding import PartitionSpec as P

CAP = 40
KC = 512
NB = 3
GAP = 1
F32 = jnp.float32
BF16 = jnp.bfloat16


def dispatch_kernel(
    n, tp, units, blocks, rp, nc, tn, fused,
    *refs,
):
    x_ref, tgt_ref, w_ref, e_ref, b_ref = refs[:5]
    if fused:
        mag_ref, hi_ref, lo_ref, out_ref = refs[5:9]
        refs, tail = refs[9:28], refs[28:]
    else:
        y_ref, sq_ref = refs[5:7]
        refs = refs[7:26]
    (
        gath, land, relay, tg, place, lhs, wbuf, acc, low, sqa, sqs, sqr,
        t_send, t_recv, send, recv, wsem, q_send, q_recv,
    ) = refs
    me = lax.axis_index("ep")
    mt = lax.axis_index("tp")
    tok = x_ref.shape[0]
    width = w_ref.shape[2]
    rank = b_ref.shape[0] // units
    rows = n * rp
    is_end = jnp.logical_or(me == 0, me == n - 1)

    def w_copy(c, u):
        slot = lax.rem(c, NB)
        return pltpu.make_async_copy(
            w_ref.at[u, pl.ds(pl.multiple_of(c * KC, KC), KC), :],
            wbuf.at[slot, pl.ds(u * KC, KC), :],
            wsem.at[slot, u],
        )

    for c in range(min(NB - 1, nc)):
        for u in range(units):
            w_copy(jnp.int32(c), u).start()

    barrier = pltpu.get_barrier_semaphore()

    def greet(d, _):
        pl.semaphore_signal(barrier, inc=1, device_id={"ep": lax.rem(me + d, n)})
        return 0

    def greet_tp(d, _):
        pl.semaphore_signal(barrier, inc=1, device_id={"tp": lax.rem(mt + d, tp)})
        return 0

    lax.fori_loop(1, n, greet, 0)
    lax.fori_loop(1, tp, greet_tp, 0)
    pl.semaphore_wait(barrier, n + tp - 2)

    def remote(src, dst, slot, s, c, to):
        return pltpu.make_async_remote_copy(
            src_ref=src, dst_ref=dst, send_sem=send.at[slot, c], recv_sem=recv.at[s, c],
            device_id={"ep": to},
        )

    def own_cols(c):
        return pl.ds(pl.multiple_of(c * KC, KC), KC)

    def own_full(c, slot, to):
        return remote(x_ref.at[:, own_cols(c)], gath.at[me, c], slot, me, c, to)

    def fwd_full(s, c, to):
        return remote(gath.at[s, c], gath.at[s, c], s, s, c, to)

    def packed(s, slot, c, to):
        return remote(relay.at[slot, c], land.at[s, c], slot, s, c, to)

    def pack(role, s, value):
        return jnp.dot(place[role, s], value, preferred_element_type=F32)

    def own_send_full(c):
        @pl.when(me < n - 2)
        def _():
            own_full(c, me, me + 1).start()

        @pl.when(me > 1)
        def _():
            own_full(c, n, me - 1).start()

    def own_send_packed(c):
        @pl.when(me == n - 2)
        def _():
            relay[me, c] = pack(1, me, x_ref[:, own_cols(c)]).astype(BF16)
            packed(me, me, c, n - 1).start()

        @pl.when(me == 1)
        def _():
            relay[n, c] = pack(2, me, x_ref[:, own_cols(c)]).astype(BF16)
            packed(me, n, c, 0).start()

    def tell(to):
        return pltpu.make_async_remote_copy(
            src_ref=tgt_ref, dst_ref=tg.at[me], send_sem=t_send.at[to], recv_sem=t_recv.at[me],
            device_id={"ep": to},
        )

    def hear(s):
        return pltpu.make_async_remote_copy(
            src_ref=tgt_ref, dst_ref=tg.at[s], send_sem=t_send.at[s], recv_sem=t_recv.at[s],
            device_id={"ep": s},
        )

    def start_tell(d, _):
        tell(lax.rem(me + d, n)).start()
        return 0

    lax.fori_loop(1, n, start_tell, 0)

    def own_all(c, _):
        own_send_full(c)
        return 0

    lax.fori_loop(0, nc, own_all, 0)
    tg[me] = tgt_ref[...]

    row = lax.broadcasted_iota(jnp.int32, (rp, tok), 0)

    def wanted(dest):
        val = jnp.full((rp, tok), -1, jnp.int32)
        for u in range(units):
            e = (dest * units + u) // blocks
            inside = jnp.logical_and(row >= u * CAP, row < (u + 1) * CAP)
            val = jnp.where(inside, row + (e * CAP - u * CAP), val)
        return val

    def build(s):
        t = tg[s]
        for role, dest in enumerate((me, n - 1, 0)):
            val = wanted(dest)
            hit = jnp.logical_or(t[0:1, :] == val, t[1:2, :] == val)
            place[role, s] = jnp.where(hit, 1.0, 0.0).astype(BF16)

    build(me)

    def own_all_packed(c, _):
        own_send_packed(c)
        return 0

    lax.fori_loop(0, nc, own_all_packed, 0)

    acc[...] = jnp.zeros_like(acc)
    low[...] = jnp.zeros_like(low)
    sqa[...] = jnp.zeros_like(sqa)

    def others(d, _):
        s = lax.rem(me + d, n)
        hear(s).wait_recv()
        build(s)
        return 0

    lax.fori_loop(1, n, others, 0)

    mrow = lax.broadcasted_iota(jnp.int32, (rp, KC), 0)

    def put(s, value):
        at = pl.ds(pl.multiple_of(s * rp, 16), rp)
        for u in range(units):
            mine = jnp.logical_and(mrow >= u * CAP, mrow < (u + 1) * CAP)
            lhs[at, pl.ds(u * KC, KC)] = jnp.where(mine, value, 0.0).astype(BF16)

    def arrive(s, c):
        @pl.when(is_end)
        def _():
            packed(s, s, c, s).wait_recv()

        @pl.when(jnp.logical_not(is_end))
        def _():
            fwd_full(s, c, s).wait_recv()

            @pl.when(s < me)
            def _():
                @pl.when(me < n - 2)
                def _():
                    fwd_full(s, c, me + 1).start()

                @pl.when(me == n - 2)
                def _():
                    relay[s, c] = pack(1, s, gath[s, c]).astype(BF16)
                    packed(s, s, c, n - 1).start()

            @pl.when(s > me)
            def _():
                @pl.when(me > 1)
                def _():
                    fwd_full(s, c, me - 1).start()

                @pl.when(me == 1)
                def _():
                    relay[s, c] = pack(2, s, gath[s, c]).astype(BF16)
                    packed(s, s, c, 0).start()

    def arrivals(c):
        def by_distance(d, _):
            k = c + (n - 1 - d) * GAP
            live = jnp.logical_and(k >= 0, k < nc)

            @pl.when(jnp.logical_and(live, me - d >= 0))
            def _():
                arrive(me - d, k)

            @pl.when(jnp.logical_and(live, me + d < n))
            def _():
                arrive(me + d, k)

            return 0

        lax.fori_loop(1, n, by_distance, 0)

    def early(i, _):
        arrivals(i - (n - 2) * GAP)
        return 0

    lax.fori_loop(0, (n - 2) * GAP, early, 0)

    def step(c, _):
        @pl.when(c + (NB - 1) < nc)
        def _():
            for u in range(units):
                w_copy(c + (NB - 1), u).start()

        arrivals(c)

        def gather_row(d, _):
            s = lax.rem(me + d, n)

            @pl.when(is_end)
            def _():
                put(s, land[s, c].astype(F32))

            @pl.when(jnp.logical_not(is_end))
            def _():
                put(s, pack(0, s, gath[s, c]))

            return 0

        lax.fori_loop(1, n, gather_row, 0)
        put(me, pack(0, me, x_ref[:, own_cols(c)]))
        lhs[pl.ds(rows, units * rank), :] = e_ref[c]
        for u in range(units):
            w_copy(c, u).wait()
        slot = lax.rem(c, NB)

        def tile(j, _):
            cols = pl.ds(pl.multiple_of(j * tn, tn), tn)
            acc[:, cols] += jnp.dot(lhs[...], wbuf[slot, :, cols], preferred_element_type=F32)
            for u in range(units):
                w = wbuf[slot, pl.ds(u * KC, KC), cols].astype(F32)
                sqa[u, :, cols] += jnp.sum((w * w).reshape(KC // 8, 8, tn), axis=0)
            return 0

        lax.fori_loop(0, width // tn, tile, 0)
        low[...] += lax.dot_general(
            lhs[...], e_ref[c], (((1,), (1,)), ((), ())), preferred_element_type=F32
        )
        return 0

    lax.fori_loop(0, nc, step, 0)

    low_rows = low[pl.ds(0, rows), :].astype(BF16)
    gram = low[pl.ds(rows, units * rank), :]

    def squares(j, _):
        cols = pl.ds(pl.multiple_of(j * tn, tn), tn)
        bf = b_ref[:, cols].astype(F32)
        inner = acc[pl.ds(rows, units * rank), cols] + jnp.dot(
            gram, bf, precision=lax.Precision.HIGHEST, preferred_element_type=F32
        )
        cross = bf * inner
        for u in range(units):
            base = jnp.sum(sqa[u, :, cols], axis=0, keepdims=True)
            extra = jnp.sum(cross[u * rank:(u + 1) * rank], axis=0, keepdims=True)
            sqs[u:u + 1, cols] = base + 4.0 * extra
        return 0

    sqs[...] = jnp.zeros_like(sqs)
    lax.fori_loop(0, width // tn, squares, 0)

    def square_copy(d):
        return pltpu.make_async_remote_copy(
            src_ref=sqs, dst_ref=sqr.at[d], send_sem=q_send.at[d], recv_sem=q_recv.at[d],
            device_id={"tp": lax.rem(mt + d, tp)},
        )

    for d in range(1, tp):
        square_copy(d).start()

    if not fused:

        def finish(j, _):
            cols = pl.ds(pl.multiple_of(j * tn, tn), tn)
            y_ref[:, cols] = (
                acc[pl.ds(0, rows), cols]
                + 2.0 * jnp.dot(low_rows, b_ref[:, cols], preferred_element_type=F32)
            ).astype(BF16)
            return 0

        lax.fori_loop(0, width // tn, finish, 0)
        for d in range(1, tp):
            square_copy(d).wait_recv()
        total = sqs[...]
        for d in range(1, tp):
            total = total + sqr[d]
        sq_ref[...] = total
    else:
        ys, got1, half, got2, outgo, back, s1, r1, s2, r2, s3, r3 = tail
        wp = width // tp
        pairs = tp // 2
        core = lax.rem(mt, 2)
        mx = mt // 2
        other = 1 - core

        def make_part(p):
            cols = pl.ds(pl.multiple_of(p * wp, 128), wp)
            ys[p] = (
                acc[pl.ds(0, rows), cols]
                + 2.0 * jnp.dot(low_rows, b_ref[:, cols], preferred_element_type=F32)
            ).astype(BF16)

        def to_core(i):
            return pltpu.make_async_remote_copy(
                src_ref=ys.at[2 * i + other], dst_ref=got1.at[i], send_sem=s1.at[i], recv_sem=r1.at[i],
                device_id={"tp": 2 * mx + other},
            )

        order = [lax.rem(mx + 1 + i, pairs) for i in range(pairs)]
        for i in order:
            make_part(2 * i + other)
            to_core(i).start()
        for i in order:
            make_part(2 * i + core)

        def span(blk):
            return pl.ds(pl.multiple_of(blk * rp, 16), rp)

        def to_chip(i, k, blk):
            return pltpu.make_async_remote_copy(
                src_ref=half.at[i, span(blk)], dst_ref=got2.at[k, span(blk)],
                send_sem=s2.at[k, blk], recv_sem=r2.at[k, blk],
                device_id={"tp": 2 * i + core},
            )

        turns = [lax.rem(me + 1 + i, n) for i in range(n)]
        for k, i in enumerate(order[:-1]):
            to_core(i).wait_recv()
            for blk in turns:
                half[i, span(blk)] = (
                    ys[2 * i + core, span(blk)].astype(F32) + got1[i, span(blk)].astype(F32)
                ).astype(BF16)
                to_chip(i, k, blk).start()
        to_core(mx).wait_recv()
        for d in range(1, tp):
            square_copy(d).wait_recv()
        mycols = pl.ds(pl.multiple_of(mt * wp, 128), wp)
        total = sqs[:, mycols]
        for d in range(1, tp):
            total = total + sqr[d, :, mycols]
        total = jnp.maximum(total[:units], 0.0)
        col_scale = mag_ref[:, mycols] / jnp.sqrt(total + 1e-06)
        orow = lax.broadcasted_iota(jnp.int32, (rp, wp), 0)
        row_scale = jnp.zeros((rp, wp), F32)
        for u in range(units):
            inside = jnp.logical_and(orow >= u * CAP, orow < (u + 1) * CAP)
            row_scale = jnp.where(inside, col_scale[u:u + 1], row_scale)

        def home(blk):
            return pltpu.make_async_remote_copy(
                src_ref=outgo.at[blk], dst_ref=back.at[me], send_sem=s3.at[blk], recv_sem=r3.at[me],
                device_id={"ep": blk},
            )

        def landed(src):
            return pltpu.make_async_remote_copy(
                src_ref=outgo.at[src], dst_ref=back.at[src], send_sem=s3.at[src], recv_sem=r3.at[src],
                device_id={"ep": src},
            )

        for t, blk in enumerate(turns):
            value = ys[mt, span(blk)].astype(F32) + got1[mx, span(blk)].astype(F32)
            for k, i in enumerate(order[:-1]):
                to_chip(i, k, blk).wait_recv()
                value = value + got2[k, span(blk)].astype(F32)
            value = (value * row_scale).astype(BF16)
            if t < n - 1:
                outgo[blk] = value
                home(blk).start()
            else:
                back[me] = value
        for i in turns[:-1]:
            landed(i).wait_recv()
        table = back[...].reshape(rows, wp)
        out_ref[...] = (
            jnp.dot(hi_ref[...], table, preferred_element_type=F32)
            + jnp.dot(lo_ref[...], table, preferred_element_type=F32)
        ).astype(BF16)
        for i in turns[:-1]:
            home(i).wait_send()
        for i in order:
            to_core(i).wait_send()
        for k, i in enumerate(order[:-1]):
            for blk in turns:
                to_chip(i, k, blk).wait_send()

    for d in range(1, tp):
        square_copy(d).wait_send()

    def done_tell(d, _):
        tell(lax.rem(me + d, n)).wait_send()
        return 0

    lax.fori_loop(1, n, done_tell, 0)

    def drain(c, _):
        @pl.when(me < n - 2)
        def _():
            own_full(c, me, me + 1).wait_send()

        @pl.when(me == n - 2)
        def _():
            packed(me, me, c, n - 1).wait_send()

        @pl.when(me > 1)
        def _():
            own_full(c, n, me - 1).wait_send()

        @pl.when(me == 1)
        def _():
            packed(me, n, c, 0).wait_send()

        def sent(s, _):
            @pl.when(jnp.logical_and(s < me, me < n - 2))
            def _():
                fwd_full(s, c, me + 1).wait_send()

            @pl.when(jnp.logical_and(s < me, me == n - 2))
            def _():
                packed(s, s, c, n - 1).wait_send()

            @pl.when(jnp.logical_and(s > me, me > 1))
            def _():
                fwd_full(s, c, me - 1).wait_send()

            @pl.when(jnp.logical_and(s > me, me == 1))
            def _():
                packed(s, s, c, 0).wait_send()

            return 0

        @pl.when(jnp.logical_not(is_end))
        def _():
            lax.fori_loop(0, n, sent, 0)

        return 0

    lax.fori_loop(0, nc, drain, 0)


def routed_products(activations, target, weight, mine, widening, n, blocks, tail_in):
    tok, feat = activations.shape
    units, _, width = weight.shape
    rank = mine.shape[2]
    rp = -(-units * CAP // 16) * 16
    nc = feat // KC
    tp = lax.axis_size("tp")
    tn = width // 3 if width % 384 == 0 else width
    rows = n * rp
    low_t = mine.reshape(units, nc, KC, rank).transpose(1, 0, 3, 2)
    diag = jnp.eye(units, dtype=BF16)
    e_all = (low_t[:, :, :, None, :] * diag[None, :, None, :, None]).reshape(
        nc, units * rank, units * KC
    )
    b_all = widening.reshape(units * rank, width)
    targets = jnp.pad(target.T, ((0, 6), (0, 0)), constant_values=-2)
    vmem = pl.BlockSpec(memory_space=pltpu.VMEM)
    wp = width // tp
    fused = len(tail_in) > 0
    if fused:
        out_shape = jax.ShapeDtypeStruct((tok, wp), BF16)
        out_specs = vmem
        tail_scratch = [
            pltpu.VMEM((tp, rows, wp), BF16),
            pltpu.VMEM((tp // 2, rows, wp), BF16),
            pltpu.VMEM((tp // 2, rows, wp), BF16),
            pltpu.VMEM((tp // 2, rows, wp), BF16),
            pltpu.VMEM((n, rp, wp), BF16),
            pltpu.VMEM((n, rp, wp), BF16),
            pltpu.SemaphoreType.DMA((tp // 2,)),
            pltpu.SemaphoreType.DMA((tp // 2,)),
            pltpu.SemaphoreType.DMA((tp // 2, n)),
            pltpu.SemaphoreType.DMA((tp // 2, n)),
            pltpu.SemaphoreType.DMA((n,)),
            pltpu.SemaphoreType.DMA((n,)),
        ]
    else:
        out_shape = (
            jax.ShapeDtypeStruct((rows, width), BF16),
            jax.ShapeDtypeStruct((8, width), F32),
        )
        out_specs = (vmem, vmem)
        tail_scratch = []
    return pl.pallas_call(
        functools.partial(dispatch_kernel, n, tp, units, blocks, rp, nc, tn, fused),
        out_shape=out_shape,
        in_specs=[vmem, vmem, pl.BlockSpec(memory_space=pl.ANY), vmem, vmem]
        + [vmem] * len(tail_in),
        out_specs=out_specs,
        scratch_shapes=[
            pltpu.VMEM((n, nc, tok, KC), BF16),
            pltpu.VMEM((n, nc, rp, KC), BF16),
            pltpu.VMEM((n + 1, nc, rp, KC), BF16),
            pltpu.VMEM((n, 8, tok), jnp.int32),
            pltpu.VMEM((3, n, rp, tok), BF16),
            pltpu.VMEM((rows + units * rank, units * KC), BF16),
            pltpu.VMEM((NB, units * KC, width), BF16),
            pltpu.VMEM((rows + units * rank, width), F32),
            pltpu.VMEM((rows + units * rank, units * rank), F32),
            pltpu.VMEM((units, 8, width), F32),
            pltpu.VMEM((8, width), F32),
            pltpu.VMEM((tp, 8, width), F32),
            pltpu.SemaphoreType.DMA((n,)),
            pltpu.SemaphoreType.DMA((n,)),
            pltpu.SemaphoreType.DMA((n + 1, nc)),
            pltpu.SemaphoreType.DMA((n, nc)),
            pltpu.SemaphoreType.DMA((NB, units)),
            pltpu.SemaphoreType.DMA((tp,)),
            pltpu.SemaphoreType.DMA((tp,)),
        ]
        + tail_scratch,
        compiler_params=pltpu.CompilerParams(
            collective_id=0, has_side_effects=True, vmem_limit_bytes=60 * 1024 * 1024
        ),
        cost_estimate=pl.CostEstimate(
            flops=2 * rows * feat * width, bytes_accessed=2 * units * feat * width, transcendentals=0
        ),
        name="routed_products",
    )(activations, targets, weight, e_all, b_all, *tail_in)


def on_device(
    activations,
    token_expert_index,
    gate_integer_weights,
    weight,
    left_reducing_matrices,
    right_widening_matrices,
    magnitude,
):
    ep_count = lax.axis_size("ep")
    tok_count = activations.shape[0]
    units_here = weight.shape[0]
    expert_list = left_reducing_matrices.shape[0]
    blocks = units_here * ep_count // expert_list
    flat = token_expert_index.reshape(-1)
    onehot = (flat[:, None] == jnp.arange(expert_list, dtype=jnp.int32)[None, :]).astype(jnp.int32)
    before = jnp.cumsum(onehot, axis=0) - onehot
    slot = jnp.sum(before * onehot, axis=1)
    target = (flat * CAP + slot).reshape(tok_count, 2)
    slot_total = expert_list * CAP
    match = jnp.arange(slot_total, dtype=jnp.int32)[:, None, None] == target[None, :, :]
    first_unit = lax.axis_index("ep") * units_here
    mine = jnp.stack(
        [
            lax.dynamic_index_in_dim(
                left_reducing_matrices, (first_unit + unit) // blocks, 0, keepdims=False
            )
            for unit in range(units_here)
        ],
        axis=0,
    )
    tp_count = lax.axis_size("tp")
    column_width = weight.shape[2]
    if (
        blocks == 1
        and tp_count % 2 == 0
        and column_width % (128 * tp_count) == 0
        and units_here * CAP % 16 == 0
    ):
        coarse = gate_integer_weights // 256 * 256
        fine = gate_integer_weights - coarse
        gates = [
            (jnp.sum(jnp.where(match, part[None], 0), axis=-1).T.astype(F32) / 65536.0).astype(BF16)
            for part in (coarse, fine)
        ]
        mixed = routed_products(
            activations, target, weight, mine, right_widening_matrices, ep_count, blocks,
            [magnitude] + gates,
        )
        return mixed.reshape(tok_count, blocks, column_width // tp_count)
    partial_rows, squares = routed_products(
        activations, target, weight, mine, right_widening_matrices, ep_count, blocks, []
    )
    total_sq = jnp.maximum(squares[:units_here], 0.0)
    col_scale = magnitude / jnp.sqrt(total_sq + 1e-06)
    gate_real = gate_integer_weights.astype(F32) / 65536.0
    combiner = jnp.sum(match.astype(F32) * gate_real[None, :, :], axis=-1).T
    summed = lax.psum_scatter(partial_rows, "tp", scatter_dimension=1, tiled=True).astype(F32)
    width = summed.shape[1]
    summed = summed.reshape(ep_count, -1, width)[:, : units_here * CAP].reshape(
        ep_count, units_here, CAP, width
    )
    scale_part = lax.dynamic_slice_in_dim(col_scale, lax.axis_index("tp") * width, width, 1)
    back = lax.all_to_all(
        (summed * scale_part[None, :, None, :]).astype(BF16),
        "ep",
        split_axis=0,
        concat_axis=0,
        tiled=True,
    ).astype(F32)
    table = (
        back.reshape(expert_list, blocks, CAP, width)
        .transpose(0, 2, 1, 3)
        .reshape(slot_total, blocks * width)
    )
    mixed = jnp.dot(combiner, table, precision=lax.Precision.HIGHEST).reshape(
        tok_count, blocks, width
    )
    return mixed.astype(BF16)


def solution(mesh):
    return jax.shard_map(
        on_device,
        mesh=mesh,
        in_specs=(
            P(("groups", "ep"), "tp"),
            P(("groups", "ep"), None),
            P(("groups", "ep"), None),
            P("ep", "tp", None),
            P(None, "tp", None),
            P("ep", None, None),
            P("ep", None),
        ),
        out_specs=P(("groups", "ep"), None, "tp"),
        check_vma=False,
    )
```

```python
import functools

import jax
import jax.numpy as jnp
from jax import lax
from jax.experimental import pallas as pl
from jax.experimental.pallas import tpu as pltpu
from jax.sharding import PartitionSpec as P

CAP = 40
KC = 1024
NB = 2
GAP = 1
F32 = jnp.float32
BF16 = jnp.bfloat16


def dispatch_kernel(
    n, tp, units, blocks, rp, nc, tn, fused,
    *refs,
):
    x_ref, tgt_ref, w_ref, e_ref, b_ref = refs[:5]
    if fused:
        mag_ref, hi_ref, lo_ref, out_ref = refs[5:9]
        refs, tail = refs[9:28], refs[28:]
    else:
        y_ref, sq_ref = refs[5:7]
        refs = refs[7:26]
    (
        gath, land, relay, tg, place, lhs, wbuf, acc, low, sqa, sqs, sqr,
        t_send, t_recv, send, recv, wsem, q_send, q_recv,
    ) = refs
    me = lax.axis_index("ep")
    mt = lax.axis_index("tp")
    tok = x_ref.shape[0]
    width = w_ref.shape[2]
    rank = b_ref.shape[0] // units
    rows = n * rp
    is_end = jnp.logical_or(me == 0, me == n - 1)

    def w_copy(c, u):
        slot = lax.rem(c, NB)
        return pltpu.make_async_copy(
            w_ref.at[u, pl.ds(pl.multiple_of(c * KC, KC), KC), :],
            wbuf.at[slot, pl.ds(u * KC, KC), :],
            wsem.at[slot, u],
        )

    for c in range(min(NB - 1, nc)):
        for u in range(units):
            w_copy(jnp.int32(c), u).start()

    barrier = pltpu.get_barrier_semaphore()

    def greet(d, _):
        pl.semaphore_signal(barrier, inc=1, device_id={"ep": lax.rem(me + d, n)})
        return 0

    def greet_tp(d, _):
        pl.semaphore_signal(barrier, inc=1, device_id={"tp": lax.rem(mt + d, tp)})
        return 0

    lax.fori_loop(1, n, greet, 0)
    lax.fori_loop(1, tp, greet_tp, 0)
    pl.semaphore_wait(barrier, n + tp - 2)

    def remote(src, dst, slot, s, c, to):
        return pltpu.make_async_remote_copy(
            src_ref=src, dst_ref=dst, send_sem=send.at[slot, c], recv_sem=recv.at[s, c],
            device_id={"ep": to},
        )

    def own_cols(c):
        return pl.ds(pl.multiple_of(c * KC, KC), KC)

    def own_full(c, slot, to):
        return remote(x_ref.at[:, own_cols(c)], gath.at[me, c], slot, me, c, to)

    def fwd_full(s, c, to):
        return remote(gath.at[s, c], gath.at[s, c], s, s, c, to)

    def packed(s, slot, c, to):
        return remote(relay.at[slot, c], land.at[s, c], slot, s, c, to)

    def pack(role, s, value):
        return jnp.dot(place[role, s], value, preferred_element_type=F32)

    def own_send_full(c):
        @pl.when(me < n - 2)
        def _():
            own_full(c, me, me + 1).start()

        @pl.when(me > 1)
        def _():
            own_full(c, n, me - 1).start()

    def own_send_packed(c):
        @pl.when(me == n - 2)
        def _():
            relay[me, c] = pack(1, me, x_ref[:, own_cols(c)]).astype(BF16)
            packed(me, me, c, n - 1).start()

        @pl.when(me == 1)
        def _():
            relay[n, c] = pack(2, me, x_ref[:, own_cols(c)]).astype(BF16)
            packed(me, n, c, 0).start()

    def tell(to):
        return pltpu.make_async_remote_copy(
            src_ref=tgt_ref, dst_ref=tg.at[me], send_sem=t_send.at[to], recv_sem=t_recv.at[me],
            device_id={"ep": to},
        )

    def hear(s):
        return pltpu.make_async_remote_copy(
            src_ref=tgt_ref, dst_ref=tg.at[s], send_sem=t_send.at[s], recv_sem=t_recv.at[s],
            device_id={"ep": s},
        )

    def start_tell(d, _):
        tell(lax.rem(me + d, n)).start()
        return 0

    lax.fori_loop(1, n, start_tell, 0)

    def own_all(c, _):
        own_send_full(c)
        return 0

    lax.fori_loop(0, nc, own_all, 0)
    tg[me] = tgt_ref[...]

    row = lax.broadcasted_iota(jnp.int32, (rp, tok), 0)

    def wanted(dest):
        val = jnp.full((rp, tok), -1, jnp.int32)
        for u in range(units):
            e = (dest * units + u) // blocks
            inside = jnp.logical_and(row >= u * CAP, row < (u + 1) * CAP)
            val = jnp.where(inside, row + (e * CAP - u * CAP), val)
        return val

    def build(s):
        t = tg[s]
        for role, dest in enumerate((me, n - 1, 0)):
            val = wanted(dest)
            hit = jnp.logical_or(t[0:1, :] == val, t[1:2, :] == val)
            place[role, s] = jnp.where(hit, 1.0, 0.0).astype(BF16)

    build(me)

    def own_all_packed(c, _):
        own_send_packed(c)
        return 0

    lax.fori_loop(0, nc, own_all_packed, 0)

    acc[...] = jnp.zeros_like(acc)
    low[...] = jnp.zeros_like(low)
    sqa[...] = jnp.zeros_like(sqa)

    def others(d, _):
        s = lax.rem(me + d, n)
        hear(s).wait_recv()
        build(s)
        return 0

    lax.fori_loop(1, n, others, 0)

    mrow = lax.broadcasted_iota(jnp.int32, (rp, KC), 0)

    def put(s, value):
        at = pl.ds(pl.multiple_of(s * rp, 16), rp)
        for u in range(units):
            mine = jnp.logical_and(mrow >= u * CAP, mrow < (u + 1) * CAP)
            lhs[at, pl.ds(u * KC, KC)] = jnp.where(mine, value, 0.0).astype(BF16)

    def arrive(s, c):
        @pl.when(is_end)
        def _():
            packed(s, s, c, s).wait_recv()

        @pl.when(jnp.logical_not(is_end))
        def _():
            fwd_full(s, c, s).wait_recv()

            @pl.when(s < me)
            def _():
                @pl.when(me < n - 2)
                def _():
                    fwd_full(s, c, me + 1).start()

                @pl.when(me == n - 2)
                def _():
                    relay[s, c] = pack(1, s, gath[s, c]).astype(BF16)
                    packed(s, s, c, n - 1).start()

            @pl.when(s > me)
            def _():
                @pl.when(me > 1)
                def _():
                    fwd_full(s, c, me - 1).start()

                @pl.when(me == 1)
                def _():
                    relay[s, c] = pack(2, s, gath[s, c]).astype(BF16)
                    packed(s, s, c, 0).start()

    def arrivals(c):
        def by_distance(d, _):
            k = c + (n - 1 - d) * GAP
            live = jnp.logical_and(k >= 0, k < nc)

            @pl.when(jnp.logical_and(live, me - d >= 0))
            def _():
                arrive(me - d, k)

            @pl.when(jnp.logical_and(live, me + d < n))
            def _():
                arrive(me + d, k)

            return 0

        lax.fori_loop(1, n, by_distance, 0)

    def early(i, _):
        arrivals(i - (n - 2) * GAP)
        return 0

    lax.fori_loop(0, (n - 2) * GAP, early, 0)

    def step(c, _):
        @pl.when(c + (NB - 1) < nc)
        def _():
            for u in range(units):
                w_copy(c + (NB - 1), u).start()

        arrivals(c)

        def gather_row(d, _):
            s = lax.rem(me + d, n)

            @pl.when(is_end)
            def _():
                put(s, land[s, c].astype(F32))

            @pl.when(jnp.logical_not(is_end))
            def _():
                put(s, pack(0, s, gath[s, c]))

            return 0

        lax.fori_loop(1, n, gather_row, 0)
        put(me, pack(0, me, x_ref[:, own_cols(c)]))
        lhs[pl.ds(rows, units * rank), :] = e_ref[c]
        for u in range(units):
            w_copy(c, u).wait()
        slot = lax.rem(c, NB)

        def tile(j, _):
            cols = pl.ds(pl.multiple_of(j * tn, tn), tn)
            acc[:, cols] += jnp.dot(lhs[...], wbuf[slot, :, cols], preferred_element_type=F32)
            for u in range(units):
                w = wbuf[slot, pl.ds(u * KC, KC), cols].astype(F32)
                sqa[u, :, cols] += jnp.sum((w * w).reshape(KC // 8, 8, tn), axis=0)
            return 0

        lax.fori_loop(0, width // tn, tile, 0)
        low[...] += lax.dot_general(
            lhs[...], e_ref[c], (((1,), (1,)), ((), ())), preferred_element_type=F32
        )
        return 0

    lax.fori_loop(0, nc, step, 0)

    low_rows = low[pl.ds(0, rows), :].astype(BF16)
    gram = low[pl.ds(rows, units * rank), :]

    def squares(j, _):
        cols = pl.ds(pl.multiple_of(j * tn, tn), tn)
        bf = b_ref[:, cols].astype(F32)
        inner = acc[pl.ds(rows, units * rank), cols] + jnp.dot(
            gram, bf, precision=lax.Precision.HIGHEST, preferred_element_type=F32
        )
        cross = bf * inner
        for u in range(units):
            base = jnp.sum(sqa[u, :, cols], axis=0, keepdims=True)
            extra = jnp.sum(cross[u * rank:(u + 1) * rank], axis=0, keepdims=True)
            sqs[u:u + 1, cols] = base + 4.0 * extra
        return 0

    sqs[...] = jnp.zeros_like(sqs)
    lax.fori_loop(0, width // tn, squares, 0)

    def square_copy(d):
        return pltpu.make_async_remote_copy(
            src_ref=sqs, dst_ref=sqr.at[d], send_sem=q_send.at[d], recv_sem=q_recv.at[d],
            device_id={"tp": lax.rem(mt + d, tp)},
        )

    for d in range(1, tp):
        square_copy(d).start()

    if not fused:

        def finish(j, _):
            cols = pl.ds(pl.multiple_of(j * tn, tn), tn)
            y_ref[:, cols] = (
                acc[pl.ds(0, rows), cols]
                + 2.0 * jnp.dot(low_rows, b_ref[:, cols], preferred_element_type=F32)
            ).astype(BF16)
            return 0

        lax.fori_loop(0, width // tn, finish, 0)
        for d in range(1, tp):
            square_copy(d).wait_recv()
        total = sqs[...]
        for d in range(1, tp):
            total = total + sqr[d]
        sq_ref[...] = total
    else:
        ys, got1, half, got2, outgo, back, s1, r1, s2, r2, s3, r3 = tail
        wp = width // tp
        pairs = tp // 2
        core = lax.rem(mt, 2)
        mx = mt // 2
        other = 1 - core

        def make_part(p):
            cols = pl.ds(pl.multiple_of(p * wp, 128), wp)
            ys[p] = (
                acc[pl.ds(0, rows), cols]
                + 2.0 * jnp.dot(low_rows, b_ref[:, cols], preferred_element_type=F32)
            ).astype(BF16)

        def to_core(i):
            return pltpu.make_async_remote_copy(
                src_ref=ys.at[2 * i + other], dst_ref=got1.at[i], send_sem=s1.at[i], recv_sem=r1.at[i],
                device_id={"tp": 2 * mx + other},
            )

        order = [lax.rem(mx + 1 + i, pairs) for i in range(pairs)]
        for i in order:
            make_part(2 * i + other)
            to_core(i).start()
        for i in order:
            make_part(2 * i + core)

        def span(blk):
            return pl.ds(pl.multiple_of(blk * rp, 16), rp)

        def to_chip(i, k, blk):
            return pltpu.make_async_remote_copy(
                src_ref=half.at[i, span(blk)], dst_ref=got2.at[k, span(blk)],
                send_sem=s2.at[k, blk], recv_sem=r2.at[k, blk],
                device_id={"tp": 2 * i + core},
            )

        turns = [lax.rem(me + 1 + i, n) for i in range(n)]
        for k, i in enumerate(order[:-1]):
            to_core(i).wait_recv()
            for blk in turns:
                half[i, span(blk)] = (
                    ys[2 * i + core, span(blk)].astype(F32) + got1[i, span(blk)].astype(F32)
                ).astype(BF16)
                to_chip(i, k, blk).start()
        to_core(mx).wait_recv()
        for d in range(1, tp):
            square_copy(d).wait_recv()
        mycols = pl.ds(pl.multiple_of(mt * wp, 128), wp)
        total = sqs[:, mycols]
        for d in range(1, tp):
            total = total + sqr[d, :, mycols]
        total = jnp.maximum(total[:units], 0.0)
        col_scale = mag_ref[:, mycols] / jnp.sqrt(total + 1e-06)
        orow = lax.broadcasted_iota(jnp.int32, (rp, wp), 0)
        row_scale = jnp.zeros((rp, wp), F32)
        for u in range(units):
            inside = jnp.logical_and(orow >= u * CAP, orow < (u + 1) * CAP)
            row_scale = jnp.where(inside, col_scale[u:u + 1], row_scale)

        def home(blk):
            return pltpu.make_async_remote_copy(
                src_ref=outgo.at[blk], dst_ref=back.at[me], send_sem=s3.at[blk], recv_sem=r3.at[me],
                device_id={"ep": blk},
            )

        def landed(src):
            return pltpu.make_async_remote_copy(
                src_ref=outgo.at[src], dst_ref=back.at[src], send_sem=s3.at[src], recv_sem=r3.at[src],
                device_id={"ep": src},
            )

        for t, blk in enumerate(turns):
            value = ys[mt, span(blk)].astype(F32) + got1[mx, span(blk)].astype(F32)
            for k, i in enumerate(order[:-1]):
                to_chip(i, k, blk).wait_recv()
                value = value + got2[k, span(blk)].astype(F32)
            value = (value * row_scale).astype(BF16)
            if t < n - 1:
                outgo[blk] = value
                home(blk).start()
            else:
                back[me] = value
        for i in turns[:-1]:
            landed(i).wait_recv()
        table = back[...].reshape(rows, wp)
        out_ref[...] = (
            jnp.dot(hi_ref[...], table, preferred_element_type=F32)
            + jnp.dot(lo_ref[...], table, preferred_element_type=F32)
        ).astype(BF16)
        for i in turns[:-1]:
            home(i).wait_send()
        for i in order:
            to_core(i).wait_send()
        for k, i in enumerate(order[:-1]):
            for blk in turns:
                to_chip(i, k, blk).wait_send()

    for d in range(1, tp):
        square_copy(d).wait_send()

    def done_tell(d, _):
        tell(lax.rem(me + d, n)).wait_send()
        return 0

    lax.fori_loop(1, n, done_tell, 0)

    def drain(c, _):
        @pl.when(me < n - 2)
        def _():
            own_full(c, me, me + 1).wait_send()

        @pl.when(me == n - 2)
        def _():
            packed(me, me, c, n - 1).wait_send()

        @pl.when(me > 1)
        def _():
            own_full(c, n, me - 1).wait_send()

        @pl.when(me == 1)
        def _():
            packed(me, n, c, 0).wait_send()

        def sent(s, _):
            @pl.when(jnp.logical_and(s < me, me < n - 2))
            def _():
                fwd_full(s, c, me + 1).wait_send()

            @pl.when(jnp.logical_and(s < me, me == n - 2))
            def _():
                packed(s, s, c, n - 1).wait_send()

            @pl.when(jnp.logical_and(s > me, me > 1))
            def _():
                fwd_full(s, c, me - 1).wait_send()

            @pl.when(jnp.logical_and(s > me, me == 1))
            def _():
                packed(s, s, c, 0).wait_send()

            return 0

        @pl.when(jnp.logical_not(is_end))
        def _():
            lax.fori_loop(0, n, sent, 0)

        return 0

    lax.fori_loop(0, nc, drain, 0)


def routed_products(activations, target, weight, mine, widening, n, blocks, tail_in):
    tok, feat = activations.shape
    units, _, width = weight.shape
    rank = mine.shape[2]
    rp = -(-units * CAP // 16) * 16
    nc = feat // KC
    tp = lax.axis_size("tp")
    tn = width
    rows = n * rp
    low_t = mine.reshape(units, nc, KC, rank).transpose(1, 0, 3, 2)
    diag = jnp.eye(units, dtype=BF16)
    e_all = (low_t[:, :, :, None, :] * diag[None, :, None, :, None]).reshape(
        nc, units * rank, units * KC
    )
    b_all = widening.reshape(units * rank, width)
    targets = jnp.pad(target.T, ((0, 6), (0, 0)), constant_values=-2)
    vmem = pl.BlockSpec(memory_space=pltpu.VMEM)
    wp = width // tp
    fused = len(tail_in) > 0
    if fused:
        out_shape = jax.ShapeDtypeStruct((tok, wp), BF16)
        out_specs = vmem
        tail_scratch = [
            pltpu.VMEM((tp, rows, wp), BF16),
            pltpu.VMEM((tp // 2, rows, wp), BF16),
            pltpu.VMEM((tp // 2, rows, wp), BF16),
            pltpu.VMEM((tp // 2, rows, wp), BF16),
            pltpu.VMEM((n, rp, wp), BF16),
            pltpu.VMEM((n, rp, wp), BF16),
            pltpu.SemaphoreType.DMA((tp // 2,)),
            pltpu.SemaphoreType.DMA((tp // 2,)),
            pltpu.SemaphoreType.DMA((tp // 2, n)),
            pltpu.SemaphoreType.DMA((tp // 2, n)),
            pltpu.SemaphoreType.DMA((n,)),
            pltpu.SemaphoreType.DMA((n,)),
        ]
    else:
        out_shape = (
            jax.ShapeDtypeStruct((rows, width), BF16),
            jax.ShapeDtypeStruct((8, width), F32),
        )
        out_specs = (vmem, vmem)
        tail_scratch = []
    return pl.pallas_call(
        functools.partial(dispatch_kernel, n, tp, units, blocks, rp, nc, tn, fused),
        out_shape=out_shape,
        in_specs=[vmem, vmem, pl.BlockSpec(memory_space=pl.ANY), vmem, vmem]
        + [vmem] * len(tail_in),
        out_specs=out_specs,
        scratch_shapes=[
            pltpu.VMEM((n, nc, tok, KC), BF16),
            pltpu.VMEM((n, nc, rp, KC), BF16),
            pltpu.VMEM((n + 1, nc, rp, KC), BF16),
            pltpu.VMEM((n, 8, tok), jnp.int32),
            pltpu.VMEM((3, n, rp, tok), BF16),
            pltpu.VMEM((rows + units * rank, units * KC), BF16),
            pltpu.VMEM((NB, units * KC, width), BF16),
            pltpu.VMEM((rows + units * rank, width), F32),
            pltpu.VMEM((rows + units * rank, units * rank), F32),
            pltpu.VMEM((units, 8, width), F32),
            pltpu.VMEM((8, width), F32),
            pltpu.VMEM((tp, 8, width), F32),
            pltpu.SemaphoreType.DMA((n,)),
            pltpu.SemaphoreType.DMA((n,)),
            pltpu.SemaphoreType.DMA((n + 1, nc)),
            pltpu.SemaphoreType.DMA((n, nc)),
            pltpu.SemaphoreType.DMA((NB, units)),
            pltpu.SemaphoreType.DMA((tp,)),
            pltpu.SemaphoreType.DMA((tp,)),
        ]
        + tail_scratch,
        compiler_params=pltpu.CompilerParams(
            collective_id=0, has_side_effects=True, vmem_limit_bytes=60 * 1024 * 1024
        ),
        cost_estimate=pl.CostEstimate(
            flops=2 * rows * feat * width, bytes_accessed=2 * units * feat * width, transcendentals=0
        ),
        name="routed_products",
    )(activations, targets, weight, e_all, b_all, *tail_in)


def on_device(
    activations,
    token_expert_index,
    gate_integer_weights,
    weight,
    left_reducing_matrices,
    right_widening_matrices,
    magnitude,
):
    ep_count = lax.axis_size("ep")
    tok_count = activations.shape[0]
    units_here = weight.shape[0]
    expert_list = left_reducing_matrices.shape[0]
    blocks = units_here * ep_count // expert_list
    flat = token_expert_index.reshape(-1)
    onehot = (flat[:, None] == jnp.arange(expert_list, dtype=jnp.int32)[None, :]).astype(jnp.int32)
    before = jnp.cumsum(onehot, axis=0) - onehot
    slot = jnp.sum(before * onehot, axis=1)
    target = (flat * CAP + slot).reshape(tok_count, 2)
    slot_total = expert_list * CAP
    match = jnp.arange(slot_total, dtype=jnp.int32)[:, None, None] == target[None, :, :]
    first_unit = lax.axis_index("ep") * units_here
    mine = jnp.stack(
        [
            lax.dynamic_index_in_dim(
                left_reducing_matrices, (first_unit + unit) // blocks, 0, keepdims=False
            )
            for unit in range(units_here)
        ],
        axis=0,
    )
    tp_count = lax.axis_size("tp")
    column_width = weight.shape[2]
    if (
        blocks == 1
        and tp_count % 2 == 0
        and column_width % (128 * tp_count) == 0
        and units_here * CAP % 16 == 0
    ):
        coarse = gate_integer_weights // 256 * 256
        fine = gate_integer_weights - coarse
        gates = [
            (jnp.sum(jnp.where(match, part[None], 0), axis=-1).T.astype(F32) / 65536.0).astype(BF16)
            for part in (coarse, fine)
        ]
        mixed = routed_products(
            activations, target, weight, mine, right_widening_matrices, ep_count, blocks,
            [magnitude] + gates,
        )
        return mixed.reshape(tok_count, blocks, column_width // tp_count)
    partial_rows, squares = routed_products(
        activations, target, weight, mine, right_widening_matrices, ep_count, blocks, []
    )
    total_sq = jnp.maximum(squares[:units_here], 0.0)
    col_scale = magnitude / jnp.sqrt(total_sq + 1e-06)
    gate_real = gate_integer_weights.astype(F32) / 65536.0
    combiner = jnp.sum(match.astype(F32) * gate_real[None, :, :], axis=-1).T
    summed = lax.psum_scatter(partial_rows, "tp", scatter_dimension=1, tiled=True).astype(F32)
    width = summed.shape[1]
    summed = summed.reshape(ep_count, -1, width)[:, : units_here * CAP].reshape(
        ep_count, units_here, CAP, width
    )
    scale_part = lax.dynamic_slice_in_dim(col_scale, lax.axis_index("tp") * width, width, 1)
    back = lax.all_to_all(
        (summed * scale_part[None, :, None, :]).astype(BF16),
        "ep",
        split_axis=0,
        concat_axis=0,
        tiled=True,
    ).astype(F32)
    table = (
        back.reshape(expert_list, blocks, CAP, width)
        .transpose(0, 2, 1, 3)
        .reshape(slot_total, blocks * width)
    )
    mixed = jnp.dot(combiner, table, precision=lax.Precision.HIGHEST).reshape(
        tok_count, blocks, width
    )
    return mixed.astype(BF16)


def solution(mesh):
    return jax.shard_map(
        on_device,
        mesh=mesh,
        in_specs=(
            P(("groups", "ep"), "tp"),
            P(("groups", "ep"), None),
            P(("groups", "ep"), None),
            P("ep", "tp", None),
            P(None, "tp", None),
            P("ep", None, None),
            P("ep", None),
        ),
        out_specs=P(("groups", "ep"), None, "tp"),
        check_vma=False,
    )
```
